32 devices in a mesh: dp: 16 (over z, y, core), ctx: 2 (over x).
Axes of the slice: x: 2, y: 2, z: 4, core: 2. Of those that a mesh axis runs over, the one named last changes fastest.
Arguments:
- inputs: bfloat16 [32, 1024, 768], P('dp', 'ctx'), may hold values from -6 to 6
- cotangent: bfloat16 [32, 1024, 768], P('dp', 'ctx'), may hold values from -6 to 6
- mixing: bfloat16 [768, 2304], P('dp'), may hold values from -0.21875 to 0.21875
- query_bias: bfloat16 [768], P('dp'), may hold values from -3 to 3
- value_bias: bfloat16 [768], P('dp'), may hold values from -3 to 3
- projection: bfloat16 [768, 768], P('dp'), may hold values from -0.875 to 0.875
- offset: bfloat16 [768], P('dp'), may hold values from -3 to 3
- middle_gain: bfloat16 [768], P('dp'), may hold values from 0.5 to 1.5
- middle_shift: bfloat16 [768], P('dp'), may hold values from -3 to 3
- expand: bfloat16 [768, 6144], P('dp'), may hold values from -0.21875 to 0.21875
- contract: bfloat16 [3072, 768], P('dp'), may hold values from -0.21875 to 0.21875
- contract_bias: bfloat16 [768], P('dp'), may hold values from -3 to 3
- final_gain: bfloat16 [768], P('dp'), may hold values from 0.5 to 1.5
- final_shift: bfloat16 [768], P('dp'), may hold values from -3 to 3
Outputs:
- result: bfloat16 [32, 1024, 768], P('dp', 'ctx')
- input_grad: bfloat16 [32, 1024, 768], P('dp', 'ctx')
- mixing_grad: float32 [768, 2304], P('dp')
- query_grad: float32 [768], P('dp')
- value_grad: float32 [768], P('dp')
- projection_grad: float32 [768, 768], P('dp')
- offset_grad: float32 [768], P('dp')
- middle_gain_grad: float32 [768], P('dp')
- middle_shift_grad: float32 [768], P('dp')
- expand_grad: float32 [768, 6144], P('dp')
- contract_grad: float32 [3072, 768], P('dp')
- contract_bias_grad: float32 [768], P('dp')
- final_gain_grad: float32 [768], P('dp')
- final_shift_grad: float32 [768], P('dp')
The draws below stay inside these ranges and needn't reach their ends.
All inputs are finite; a program needn't handle non-finite values.
Results may differ from the reference program's by a relative error of at most 0.03.
Values may be sent and summed in bfloat16 or wider, within the bound.
A program may use at most 320 MiB of HBM per device.

```python
import math
import jax
import jax.numpy as jnp
from jax import lax

D = 768
HEADS = 12
HEAD_DIM = 64
FF = 3072
SEQ_LEN = 1024
BATCH = 32


def with_spikes(values, stream_key, source, target, blocks, factor):
    def block_of(position):
        return (jnp.arange(values.shape[position]) // (values.shape[position] // blocks)).reshape((-1,) + (1,) * (values.ndim - 1 - position))

    first = jax.random.permutation(stream_key, blocks)[block_of(target)]
    far = (block_of(target) + blocks // 2) % blocks
    return jnp.where((block_of(source) == first) | (block_of(source) == far), factor * values, values)


def block_scale(rng, shape, cuts, smallest, top_value):
    loudness, own = 1.0, jax.random.fold_in(rng, 6)
    for axis_at, blocks in cuts:
        steps = jnp.exp(jax.random.uniform(jax.random.fold_in(own, axis_at), (blocks,), jnp.float32, smallest / len(cuts), top_value / len(cuts)))
        loudness = loudness * jnp.repeat(steps, shape[axis_at] // blocks).reshape([-1 if axis == axis_at else 1 for axis in range(len(shape))])
    return loudness


def noise(stream_key, shape, spread, most, shards=(), kind=jnp.bfloat16):
    values = spread * jax.random.normal(stream_key, shape, jnp.float32)
    if shards:
        values = values * block_scale(stream_key, shape, shards, -0.22, 0.18)
    return jnp.clip(values, -most, most).astype(kind)


def heavy_noise(own_key, extent, deviation, bound, pieces, heavy, kind=jnp.bfloat16):
    result = deviation * jax.random.normal(own_key, extent, jnp.float32)
    if pieces:
        result = result * block_scale(own_key, extent, pieces, -0.22, 0.18)
    return jnp.clip(with_spikes(result, jax.random.fold_in(own_key, 3), *heavy), -bound, bound).astype(kind)


def setup_inputs(seed: int = 0) -> dict:
    arg_keys = jax.random.split(jax.random.key(seed), 15)
    inputs = heavy_noise(arg_keys[0], (BATCH, SEQ_LEN, D), 1.0, 6.0, ((0, 16), (1, 2)), (0, 2, 16, 2.0))
    cotangent = heavy_noise(arg_keys[1], (BATCH, SEQ_LEN, D), 1.0, 6.0, ((0, 16), (1, 2)), (0, 2, 16, 2.0))
    mixing = noise(arg_keys[2], (D, 3 * D), D ** -0.5, 0.21875, ((0, 16),))
    query_bias = noise(arg_keys[3], (D,), 0.5, 3.0, ((0, 16),))
    value_bias = noise(arg_keys[4], (D,), 0.5, 3.0, ((0, 16),))
    projection = noise(arg_keys[5], (D, D), (D // 16) ** -0.5, 0.875, ((0, 16),))
    offset = noise(arg_keys[6], (D,), 0.5, 3.0, ((0, 16),))
    middle_gain = jnp.clip(1.0 + 0.1 * jax.random.normal(arg_keys[7], (D,), jnp.float32), 0.5, 1.5).astype(jnp.bfloat16)
    middle_shift = noise(arg_keys[8], (D,), 0.5, 3.0, ((0, 16),))
    expand = noise(arg_keys[9], (D, 2 * FF), D ** -0.5, 0.21875, ((0, 16),))
    contract = noise(arg_keys[10], (FF, D), (FF // 4) ** -0.5, 0.21875, ((0, 16),))
    contract_bias = noise(arg_keys[11], (D,), 0.5, 3.0, ((0, 16),))
    final_gain = jnp.clip(1.0 + 0.1 * jax.random.normal(arg_keys[12], (D,), jnp.float32), 0.5, 1.5).astype(jnp.bfloat16)
    final_shift = noise(arg_keys[13], (D,), 0.5, 3.0, ((0, 16),))
    return {"inputs": inputs, "cotangent": cotangent, "mixing": mixing, "query_bias": query_bias, "value_bias": value_bias, "projection": projection, "offset": offset, "middle_gain": middle_gain, "middle_shift": middle_shift, "expand": expand, "contract": contract, "contract_bias": contract_bias, "final_gain": final_gain, "final_shift": final_shift}


@jax.custom_vjp
def low(v):
    return lax.optimization_barrier(v.astype(jnp.bfloat16)).astype(jnp.float32)

@jax.custom_vjp
def low_back(v):
    return v

def low_keep(v):
    return (low(v), None)

def low_pass(kept, grad):
    return (grad,)

def back_keep(v):
    return (v, None)

def back_low(kept, grad):
    return (low(grad),)
low.defvjp(low_keep, low_pass)
low_back.defvjp(back_keep, back_low)
EPSILON = 1e-12

def alibi_slopes(count):
    power = 2 ** int(math.floor(math.log2(count)))
    first = [2.0 ** (-8.0 * (index + 1) / power) for index in range(power)]
    extra = [2.0 ** (-4.0 * (2 * index + 1) / power) for index in range(count - power)]
    return jnp.array(first + extra, jnp.float32)

def layer_norm(value, gain, shift):
    mean = lax.optimization_barrier(jnp.mean(value, axis=-1, keepdims=True))
    centred = value - mean
    variance = lax.optimization_barrier(jnp.mean(centred * centred, axis=-1, keepdims=True))
    return centred * lax.rsqrt(variance + EPSILON) * gain + shift

def matmul(left, right):
    return jnp.dot(left, right, precision=lax.Precision.HIGHEST)

def forward(sequence, mixing, query_bias, value_bias, projection, offset, middle_gain, middle_shift, expand, contract, contract_bias, final_gain, final_shift):
    length, width = sequence.shape
    bias = jnp.concatenate([query_bias, jnp.zeros_like(query_bias), value_bias])
    mixed = low_back(low(matmul(sequence, mixing) + bias))
    queries = mixed[:, :width].reshape(length, HEADS, HEAD_DIM)
    keys = mixed[:, width:2 * width].reshape(length, HEADS, HEAD_DIM)
    values = mixed[:, 2 * width:].reshape(length, HEADS, HEAD_DIM)
    raw = jnp.einsum('qhd,khd->hqk', queries, keys, precision=lax.Precision.HIGHEST) * HEAD_DIM ** (-0.5)
    raw = low_back(raw)
    positions = jnp.arange(length, dtype=jnp.int32)
    distance = jnp.abs(positions[:, None] - positions[None, :]).astype(jnp.float32)
    scores = raw - alibi_slopes(HEADS)[:, None, None] * distance[None]
    shifted = scores - lax.optimization_barrier(jnp.max(scores, axis=-1, keepdims=True))
    weights = jnp.exp(shifted)
    probs = low(weights / lax.optimization_barrier(jnp.sum(weights, axis=-1, keepdims=True)))
    attended = jnp.einsum('hqk,khd->qhd', probs, values, precision=lax.Precision.HIGHEST).reshape(length, width)
    attended = low_back(low(attended))
    branch = low_back(matmul(attended, projection) + offset)
    first = layer_norm(sequence + branch, middle_gain, middle_shift)
    gate_up = low_back(matmul(low(first), expand))
    half = gate_up.shape[1] // 2
    hidden = jax.nn.gelu(gate_up[:, :half], approximate=False) * gate_up[:, half:]
    down = low_back(matmul(low(hidden), contract) + contract_bias)
    return layer_norm(first + down, final_gain, final_shift)

def reference(inputs, cotangent, mixing, query_bias, value_bias, projection, offset, middle_gain, middle_shift, expand, contract, contract_bias, final_gain, final_shift):
    weights = tuple((item.astype(jnp.float32) for item in (mixing, query_bias, value_bias, projection, offset, middle_gain, middle_shift, expand, contract, contract_bias, final_gain, final_shift)))
    starting = tuple((jnp.zeros(item.shape, jnp.float32) for item in weights))

    def one_sequence(totals, pair):
        sequence, grad_out = pair
        output, pullback = jax.vjp(forward, sequence.astype(jnp.float32), *weights)
        grads = pullback(grad_out.astype(jnp.float32))
        summed = tuple((total + grad for total, grad in zip(totals, grads[1:])))
        return (summed, (output.astype(jnp.bfloat16), grads[0].astype(jnp.bfloat16)))
    totals, (outputs, input_grads) = lax.scan(one_sequence, starting, (inputs, cotangent))
    return (outputs, input_grads, totals[0], totals[1], totals[2], totals[3], totals[4], totals[5], totals[6], totals[7], totals[8], totals[9], totals[10], totals[11])
```

```python
from functools import partial
import math

import jax
import jax.numpy as jnp
from jax import lax
from jax.experimental import pallas as pl
from jax.experimental.pallas import tpu as pltpu
from jax.sharding import PartitionSpec as P

HEADS = 12
HEAD_DIM = 64


EPSILON = 1e-12


def for_sending(x):
    return jax.tree.map(lambda a: a.astype(jnp.bfloat16) if a.dtype == jnp.float32 else a, x)


def alibi_slopes(count):
    power = 2 ** int(math.floor(math.log2(count)))
    first = [2.0 ** (-8.0 * (index + 1) / power) for index in range(power)]
    extra = [2.0 ** (-4.0 * (2 * index + 1) / power) for index in range(count - power)]
    return jnp.array(first + extra, jnp.float32)


def product(left, right):
    return jnp.dot(left, right, preferred_element_type=jnp.float32)


def product_tn(left, right):
    return lax.dot_general(
        left, right, (((0,), (0,)), ((), ())), preferred_element_type=jnp.float32
    )


def product_nt(left, right):
    return lax.dot_general(
        left, right, (((1,), (1,)), ((), ())), preferred_element_type=jnp.float32
    )


def norm_forward(value, gain, shift):
    mean = jnp.mean(value, axis=-1, keepdims=True)
    centred = value - mean
    factor = lax.rsqrt(jnp.mean(centred * centred, axis=-1, keepdims=True) + EPSILON)
    normed = centred * factor
    return (normed * gain + shift, normed, factor)


def norm_backward(grad, normed, factor, gain):
    scaled = grad * gain
    inner = scaled - jnp.mean(scaled, axis=-1, keepdims=True)
    inner = inner - normed * jnp.mean(scaled * normed, axis=-1, keepdims=True)
    return (inner * factor, jnp.sum(grad * normed, axis=0), jnp.sum(grad, axis=0))


def geglu(gate_up):
    half = gate_up.shape[1] // 2
    return jax.nn.gelu(gate_up[:, :half], approximate=False) * gate_up[:, half:]


def score_block(queries, keys, query_pos, slopes, factor):
    raw = jnp.einsum("qhd,khd->hqk", queries, keys, preferred_element_type=jnp.float32) * factor
    key_pos = lax.iota(jnp.int32, keys.shape[0])
    distance = jnp.abs(query_pos[:, None] - key_pos[None, :]).astype(jnp.float32)
    return raw - slopes[:, None, None] * distance[None]


def attend_piece(carry, piece, start, queries, query_pos, slopes, factor):
    total, top, mass = carry
    keys, values = piece
    count = keys.shape[0]
    keys = keys.reshape(count, HEADS, HEAD_DIM)
    values = values.reshape(count, HEADS, HEAD_DIM)
    scores = score_block(queries, keys, query_pos, slopes, factor)
    new_top = jnp.max(scores, axis=-1)
    fade = jnp.exp(top - new_top)
    weights = jnp.exp(scores - new_top[..., None])
    mass = mass * fade + jnp.sum(weights, axis=-1)
    total = total * fade[..., None] + jnp.einsum(
        "hqk,khd->hqd", weights.astype(jnp.bfloat16), values, preferred_element_type=jnp.float32
    )
    return (total, new_top, mass)


def attend_back(carry, piece, start, queries, grad_out, delta, log_mass, query_pos, slopes, factor):
    keys, values = piece
    count = keys.shape[0]
    width = keys.shape[1]
    keys = keys.reshape(count, HEADS, HEAD_DIM)
    values = values.reshape(count, HEADS, HEAD_DIM)
    scores = score_block(queries, keys, query_pos, slopes, factor)
    probs = jnp.exp(scores - log_mass[..., None])
    grad_probs = jnp.einsum("qhd,khd->hqk", grad_out, values, preferred_element_type=jnp.float32)
    grad_scores = (probs * (grad_probs - delta[..., None])).astype(jnp.bfloat16)
    grad_query = (
        jnp.einsum("hqk,khd->qhd", grad_scores, keys, preferred_element_type=jnp.float32) * factor
    )
    piece_keys = (
        jnp.einsum("hqk,qhd->khd", grad_scores, queries, preferred_element_type=jnp.float32)
        * factor
    ).reshape(count, width)
    piece_values = jnp.einsum(
        "hqk,qhd->khd", probs.astype(jnp.bfloat16), grad_out, preferred_element_type=jnp.float32
    ).reshape(count, width)
    return (grad_query, piece_keys, piece_values)


def one_batch(sequence, grad_out, full, query_pos, slopes, factor, length):
    (
        mixing,
        query_bias,
        value_bias,
        projection,
        offset,
        middle_gain,
        middle_shift,
        expand,
        contract,
        contract_bias,
        final_gain,
        final_shift,
    ) = full
    block, width = sequence.shape
    bias = jnp.concatenate([query_bias, jnp.zeros_like(query_bias), value_bias]).astype(jnp.float32)
    mixed = (product(sequence, mixing) + bias).astype(jnp.bfloat16)
    queries = mixed[:, :width].reshape(block, HEADS, HEAD_DIM)
    keys = mixed[:, width : 2 * width]
    values = mixed[:, 2 * width :]
    starting = (
        jnp.zeros((HEADS, block, HEAD_DIM), jnp.float32),
        jnp.full((HEADS, block), -jnp.inf, jnp.float32),
        jnp.zeros((HEADS, block), jnp.float32),
    )
    fold_forward = partial(
        attend_piece, queries=queries, query_pos=query_pos, slopes=slopes, factor=factor
    )
    total, top, mass = fold_forward(
        starting,
        (
            lax.all_gather(keys, "ctx", axis=0, tiled=True),
            lax.all_gather(values, "ctx", axis=0, tiled=True),
        ),
        jnp.int32(0),
    )
    attended = total / mass[..., None]
    log_mass = top + jnp.log(mass)
    attended_low = jnp.transpose(attended, (1, 0, 2)).reshape(block, width).astype(jnp.bfloat16)
    branch = product(attended_low, projection) + offset.astype(jnp.float32)
    middle_gain_f = middle_gain.astype(jnp.float32)
    first, normed_one, factor_one = norm_forward(
        sequence.astype(jnp.float32) + branch, middle_gain_f, middle_shift.astype(jnp.float32)
    )
    first_low = first.astype(jnp.bfloat16)
    gate_up = product(first_low, expand)
    hidden, geglu_back = jax.vjp(geglu, gate_up)
    hidden_low = hidden.astype(jnp.bfloat16)
    down = product(hidden_low, contract) + contract_bias.astype(jnp.float32)
    final_gain_f = final_gain.astype(jnp.float32)
    output, normed_two, factor_two = norm_forward(
        first + down, final_gain_f, final_shift.astype(jnp.float32)
    )
    grad_second, grad_final_gain, grad_final_shift = norm_backward(
        grad_out.astype(jnp.float32), normed_two, factor_two, final_gain_f
    )
    grad_down = grad_second.astype(jnp.bfloat16)
    grad_contract_bias = jnp.sum(grad_down.astype(jnp.float32), axis=0)
    grad_contract = product_tn(hidden_low, grad_down)
    grad_hidden = product_nt(grad_down, contract)
    grad_gate_up = geglu_back(grad_hidden)[0].astype(jnp.bfloat16)
    grad_expand = product_tn(first_low, grad_gate_up)
    grad_first = grad_second + product_nt(grad_gate_up, expand)
    grad_input_sum, grad_middle_gain, grad_middle_shift = norm_backward(
        grad_first, normed_one, factor_one, middle_gain_f
    )
    grad_branch = grad_input_sum.astype(jnp.bfloat16)
    grad_offset = jnp.sum(grad_branch.astype(jnp.float32), axis=0)
    grad_projection = product_tn(attended_low, grad_branch)
    grad_attended = (
        product_nt(grad_branch, projection).astype(jnp.bfloat16).reshape(block, HEADS, HEAD_DIM)
    )
    delta = jnp.einsum("qhd,hqd->hq", grad_attended.astype(jnp.float32), attended)
    starting_back = (
        jnp.zeros((block, HEADS, HEAD_DIM), jnp.float32),
        jnp.zeros((length, width), jnp.float32),
        jnp.zeros((length, width), jnp.float32),
    )
    fold_back = partial(
        attend_back,
        queries=queries,
        grad_out=grad_attended,
        delta=delta,
        log_mass=log_mass,
        query_pos=query_pos,
        slopes=slopes,
        factor=factor,
    )
    grad_query, grad_keys_all, grad_values_all = fold_back(
        starting_back,
        (
            lax.all_gather(keys, "ctx", axis=0, tiled=True),
            lax.all_gather(values, "ctx", axis=0, tiled=True),
        ),
        jnp.int32(0),
    )
    grad_keys, grad_values = (
        lax.psum_scatter(
            grad_keys_all.astype(jnp.bfloat16), "ctx", scatter_dimension=0, tiled=True
        ).astype(jnp.float32),
        lax.psum_scatter(
            grad_values_all.astype(jnp.bfloat16), "ctx", scatter_dimension=0, tiled=True
        ).astype(jnp.float32),
    )
    grad_mixed = jnp.concatenate(
        [grad_query.reshape(block, width), grad_keys, grad_values], axis=1
    ).astype(jnp.bfloat16)
    grad_mixed_f = grad_mixed.astype(jnp.float32)
    grad_query_bias = jnp.sum(grad_mixed_f[:, :width], axis=0)
    grad_value_bias = jnp.sum(grad_mixed_f[:, 2 * width :], axis=0)
    grad_mixing = product_tn(sequence, grad_mixed)
    grad_input = grad_input_sum + product_nt(grad_mixed, mixing)
    grads = (
        grad_mixing,
        grad_query_bias,
        grad_value_bias,
        grad_projection,
        grad_offset,
        grad_middle_gain,
        grad_middle_shift,
        grad_expand,
        grad_contract,
        grad_contract_bias,
        grad_final_gain,
        grad_final_shift,
    )
    return (output.astype(jnp.bfloat16), grad_input.astype(jnp.bfloat16), grads)


def body(
    inputs,
    cotangent,
    mixing,
    query_bias,
    value_bias,
    projection,
    offset,
    middle_gain,
    middle_shift,
    expand,
    contract,
    contract_bias,
    final_gain,
    final_shift,
):
    shards = (
        mixing,
        query_bias,
        value_bias,
        projection,
        offset,
        middle_gain,
        middle_shift,
        expand,
        contract,
        contract_bias,
        final_gain,
        final_shift,
    )
    batches, block, width = inputs.shape
    length = block * lax.axis_size("ctx")
    query_pos = lax.axis_index("ctx") * block + lax.iota(jnp.int32, block)
    slopes = alibi_slopes(HEADS)
    factor = HEAD_DIM ** (-0.5)
    totals = None
    outputs = []
    input_grads = []
    for index in range(batches):
        full = (
            lax.all_gather(shards[0], "dp", axis=0, tiled=True),
            lax.all_gather(shards[1], "dp", axis=0, tiled=True),
            lax.all_gather(shards[2], "dp", axis=0, tiled=True),
            lax.all_gather(shards[3], "dp", axis=0, tiled=True),
            lax.all_gather(shards[4], "dp", axis=0, tiled=True),
            lax.all_gather(shards[5], "dp", axis=0, tiled=True),
            lax.all_gather(shards[6], "dp", axis=0, tiled=True),
            lax.all_gather(shards[7], "dp", axis=0, tiled=True),
            lax.all_gather(shards[8], "dp", axis=0, tiled=True),
            lax.all_gather(shards[9], "dp", axis=0, tiled=True),
            lax.all_gather(shards[10], "dp", axis=0, tiled=True),
            lax.all_gather(shards[11], "dp", axis=0, tiled=True),
        )
        output, grad_input, grads = one_batch(
            inputs[index], cotangent[index], full, query_pos, slopes, factor, length
        )
        outputs.append(output)
        input_grads.append(grad_input)
        if totals is None:
            totals = grads
        else:
            totals = tuple((total + grad for total, grad in zip(totals, grads)))
    totals = jax.tree.map(
        lambda part: part.astype(jnp.float32),
        lax.psum_scatter(for_sending(totals), "dp", scatter_dimension=0, tiled=True),
    )
    final = jax.tree.map(
        lambda part: part.astype(jnp.float32), lax.psum(for_sending(totals), "ctx")
    )
    return (
        jnp.stack(outputs),
        jnp.stack(input_grads),
        final[0],
        final[1],
        final[2],
        final[3],
        final[4],
        final[5],
        final[6],
        final[7],
        final[8],
        final[9],
        final[10],
        final[11],
    )


BF = jnp.bfloat16
F32 = jnp.float32
SDS = jax.ShapeDtypeStruct
MESH = pl.DeviceIdType.MESH
HBM = pl.BlockSpec(memory_space=pl.ANY)
VM = pl.BlockSpec(memory_space=pltpu.VMEM)
NZ = 4
LOG2E = 1.4426950408889634
SLOPES = [2.0 ** (-(m + 1)) for m in range(8)] + [2.0 ** (-0.5 * (2 * m + 1)) for m in range(4)]
RB = 256


class Place:
    def __init__(self):
        self.d = lax.axis_index("dp")
        self.x = lax.axis_index("ctx")
        self.z = self.d // 4
        self.y = lax.rem(self.d // 2, 2)
        self.c = lax.rem(self.d, 2)
        self.sib = (self.d + 1 - 2 * self.c, self.x)
        self.xn = (self.d, 1 - self.x)
        self.yn = (self.block(1, 0), self.x)
        self.zn = [None] + [(self.block(0, k), self.x) for k in range(1, NZ)]

    def block(self, j, k):
        row = self.y if j == 0 else 1 - self.y
        return lax.rem(self.z + k, NZ) * 4 + row * 2 + self.c

    def greet(self):
        bar = pltpu.get_barrier_semaphore()
        peers = [self.sib, self.xn, self.yn] + self.zn[1:]
        for peer in peers:
            pl.semaphore_signal(bar, inc=1, device_id=peer, device_id_type=MESH)
        pl.semaphore_wait(bar, len(peers))


class Sems:
    def __init__(self, ref):
        self.ref = ref
        self.names = {}

    def at(self, side, *name):
        index = self.names.setdefault(name, len(self.names))
        return self.ref.at[side, index]


def landed(ref, sem):
    pltpu.make_async_copy(ref, ref, sem).wait()


class Gather:
    Z = (1, 3, 2)
    Y = (0, 1, 3, 2)

    def __init__(self, place, sems, tag, shard, full, split=False):
        self.p, self.sems, self.tag, self.shard, self.full, self.split = place, sems, tag, shard, full, split
        self.r = shard.shape[0]
        self.sent = []

    def rows(self, d):
        return pl.ds(pl.multiple_of(d * self.r, 16), self.r)

    def dst(self, d, part):
        if not self.split:
            return self.full.at[self.rows(d)]
        return self.full.at[self.p.x if part == 0 else 1 - self.p.x, self.rows(d)]

    def src(self, part):
        if not self.split:
            return self.shard
        half = self.shard.shape[1] // 2
        side = self.p.x if part == 0 else 1 - self.p.x
        return self.shard.at[:, pl.ds(pl.multiple_of(side * half, 128), half)]

    def send(self, out, arrive, d, to, part=0, own=False):
        dst = self.dst(d, part)
        copy = pltpu.make_async_remote_copy(
            src_ref=self.src(part) if own else dst,
            dst_ref=dst,
            send_sem=self.sems.at(0, self.tag, *out),
            recv_sem=self.sems.at(1, self.tag, *arrive),
            device_id=to,
            device_id_type=MESH,
        )
        copy.start()
        self.sent.append(copy)

    def wait(self, name, d, part=0):
        landed(self.dst(d, part), self.sems.at(1, self.tag, *name))

    def start(self):
        p = self.p
        self.local = []
        for part in range(2 if self.split else 1):
            copy = pltpu.make_async_copy(
                self.src(part), self.dst(p.d, part), self.sems.at(0, self.tag, "local", part)
            )
            copy.start()
            self.local.append(copy)
        for k in self.Z:
            self.send(("z", k), ("z", NZ - k), p.d, p.zn[k], own=True)
        self.send(("y", 0), ("y", 0), p.d, p.yn, own=True)
        for part in range(2 if self.split else 1):
            self.send(("s", 0, 0, part), ("s", 0, 0, part), p.d, p.sib, part, own=True)

    def after_z(self, k):
        d = self.p.block(0, k)
        self.wait(("z", k), d)
        self.send(("y", k), ("y", k), d, self.p.yn)
        if self.split:
            self.send(("x", 0, k), ("x", 0, k), d, self.p.xn)
        self.send(("s", 0, k, 0), ("s", 0, k, 0), d, self.p.sib)

    def after_y(self, k):
        d = self.p.block(1, k)
        self.wait(("y", k), d)
        if self.split:
            self.send(("x", 1, k), ("x", 1, k), d, self.p.xn)
        self.send(("s", 1, k, 0), ("s", 1, k, 0), d, self.p.sib)

    def after_x(self, j, k):
        d = self.p.block(j, k)
        self.wait(("x", j, k), d, 1)
        self.send(("s", j, k, 1), ("s", j, k, 1), d, self.p.sib, 1)

    def along_z(self):
        return [partial(self.after_z, k) for k in self.Z]

    def along_y(self):
        return [partial(self.after_y, k) for k in self.Y]

    def along_x(self):
        return [partial(self.after_x, 0, k) for k in self.Z] + [partial(self.after_x, 1, k) for k in self.Y]

    def finish(self):
        p = self.p
        for copy in self.local:
            copy.wait()
        for j in range(2):
            for k in range(NZ):
                for part in range(2 if self.split else 1):
                    self.wait(("s", j, k, part), p.block(j, k) + 1 - 2 * p.c, part)
        for copy in self.sent:
            copy.wait_send()


class Swap:
    def __init__(self, place, sems, tag, halves, whole):
        p = place
        size = halves.shape[1]
        mine = whole.at[pl.ds(pl.multiple_of(p.x * size, 16), size)]
        self.other = whole.at[pl.ds(pl.multiple_of((1 - p.x) * size, 16), size)]
        self.local = pltpu.make_async_copy(halves.at[p.x], mine, sems.at(0, tag, "local"))
        self.copy = pltpu.make_async_remote_copy(
            src_ref=halves.at[1 - p.x],
            dst_ref=mine,
            send_sem=sems.at(0, tag, "out"),
            recv_sem=sems.at(1, tag, "out"),
            device_id=p.xn,
            device_id_type=MESH,
        )
        self.sem = sems.at(1, tag, "out")

    def start(self):
        self.copy.start()
        self.local.start()

    def finish(self):
        self.local.wait()
        landed(self.other, self.sem)
        self.copy.wait_send()


class SwapBack:
    def __init__(self, place, sems, tag, whole, halves):
        p = place
        size = halves.shape[1]
        self.local = pltpu.make_async_copy(
            whole.at[pl.ds(pl.multiple_of(p.x * size, 16), size)], halves.at[p.x], sems.at(0, tag, "local")
        )
        self.copy = pltpu.make_async_remote_copy(
            src_ref=whole.at[pl.ds(pl.multiple_of((1 - p.x) * size, 16), size)],
            dst_ref=halves.at[p.x],
            send_sem=sems.at(0, tag, "out"),
            recv_sem=sems.at(1, tag, "out"),
            device_id=p.xn,
            device_id_type=MESH,
        )
        self.other = halves.at[1 - p.x]
        self.sem = sems.at(1, tag, "out")

    def start(self):
        self.copy.start()
        self.local.start()

    def finish(self):
        self.local.wait()
        landed(self.other, self.sem)
        self.copy.wait_send()


def run(steps):
    for step in steps:
        step()


def gather_kernel(inp, cot, small, mix, expand, contract, proj,
                  xs, cs, small_all, mix_all, expand_all, contract_all, proj_all, sem_ref):
    p = Place()
    sems = Sems(sem_ref)
    s = Gather(p, sems, "small", small, small_all)
    m = Gather(p, sems, "mix", mix, mix_all)
    e = Gather(p, sems, "expand", expand, expand_all, split=True)
    c = Gather(p, sems, "contract", contract, contract_all)
    r = Gather(p, sems, "proj", proj, proj_all)
    ins = Swap(p, sems, "in", inp, xs)
    cts = Swap(p, sems, "cot", cot, cs)
    p.greet()
    s.start()
    m.start()
    ins.start()
    run(s.along_z() + m.along_z())
    e.start()
    run(s.along_y() + m.along_y())
    run(e.along_z())
    c.start()
    r.start()
    s.finish()
    m.finish()
    ins.finish()
    run(e.along_y() + c.along_z() + r.along_z())
    cts.start()
    run(e.along_x() + c.along_y() + r.along_y())
    for g in (e, c, r, cts):
        g.finish()


def gather(inp, cot, small, mix, expand, contract, proj):
    n = lax.axis_size("dp")
    two, half, width = inp.shape
    seq = SDS((two * half, width), BF)
    shapes = (
        seq,
        seq,
        SDS((n * small.shape[0], width), BF),
        SDS((n * mix.shape[0], mix.shape[1]), BF),
        SDS((2, n * expand.shape[0], expand.shape[1] // 2), BF),
        SDS((n * contract.shape[0], width), BF),
        SDS((n * proj.shape[0], width), BF),
    )
    return pl.pallas_call(
        gather_kernel,
        out_shape=shapes,
        in_specs=[HBM] * 7,
        out_specs=(HBM,) * 7,
        scratch_shapes=[pltpu.SemaphoreType.DMA((2, 160))],
        compiler_params=pltpu.CompilerParams(
            collective_id=0, has_side_effects=True, vmem_limit_bytes=16 << 20
        ),
    )(inp, cot, small, mix, expand, contract, proj)


def attend_kernel(x_ref, mix_ref, small_ref, mixed_ref, e_hbm, att_ref, linv_ref, vec_ref, far, bias, ebuf, esem):
    length, width = x_ref.shape
    total = small_ref[0:16].astype(F32)
    for block in range(1, small_ref.shape[0] // 16):
        total += small_ref[block * 16 : block * 16 + 16].astype(F32)
    vec_ref[...] = total

    def project(i, _):
        cols = pl.ds(pl.multiple_of(i * 256, 256), 256)
        out = product(x_ref[...], mix_ref[:, cols])
        here = pl.ds(pl.multiple_of(lax.rem(i, 3) * 256, 256), 256)
        out += jnp.where(i < 3, vec_ref[0:1, here], jnp.where(i < 6, 0.0, vec_ref[1:2, here]))
        out *= jnp.where(i < 3, HEAD_DIM**-0.5 * LOG2E, 1.0)
        mixed_ref[:, cols] = out.astype(BF)
        return 0

    lax.fori_loop(0, 9, project, 0)
    row = lax.broadcasted_iota(jnp.int32, far.shape, 0)
    col = lax.broadcasted_iota(jnp.int32, far.shape, 1)
    far[...] = jnp.abs(row - (length - 256) - col).astype(F32)
    lane = lax.broadcasted_iota(jnp.int32, (1, 128), 1)

    def write(head, slot):
        return pltpu.make_async_copy(ebuf.at[slot], e_hbm.at[head], esem.at[slot])

    def pair(i, _):
        q = mixed_ref[:, pl.ds(pl.multiple_of(i * 128, 128), 128)]
        k = mixed_ref[:, pl.ds(pl.multiple_of(width + i * 128, 128), 128)]
        v = mixed_ref[:, pl.ds(pl.multiple_of(2 * width + i * 128, 128), 128)]
        qt = q.T
        vt = v.T
        for side in range(2):
            head = 2 * i + side
            slope = jnp.float32(0)
            for index in range(6):
                slope = jnp.where(i == index, jnp.float32(SLOPES[2 * index + side] * LOG2E), slope)
            bias[...] = far[...] * slope

            @pl.when(i > 0)
            def _():
                write(0, side).wait()

            mine = (lane < 64) == (side == 0)
            keys = jnp.where(mine, k, jnp.zeros_like(k))
            values = jnp.concatenate([vt[side * 64 : side * 64 + 64], jnp.ones((16, length), BF)], axis=0)
            for b in range(length // 256):
                cols = slice(b * 256, b * 256 + 256)
                first = length - 256 - b * 256
                s = product(keys, qt[:, cols]) - bias[first : first + length, :]
                e = jnp.exp2(s - jnp.max(s, axis=0, keepdims=True)).astype(BF)
                ebuf[side, :, cols] = e
                out = product(values, e)
                inv = 1.0 / out[64:65]
                linv_ref[pl.ds(head, 1), cols] = inv
                att_ref[pl.ds(pl.multiple_of(head * 64, 64), 64), cols] = (out[:64] * inv).astype(BF)
            write(head, side).start()
        return 0

    lax.fori_loop(0, 6, pair, 0)
    for side in range(2):
        write(0, side).wait()


def attend(x, mix, small):
    length, width = x.shape
    return pl.pallas_call(
        attend_kernel,
        out_shape=(
            SDS((length, 3 * width), BF),
            SDS((HEADS, length, length), BF),
            SDS((width, length), BF),
            SDS((16, length), F32),
            SDS((16, width), F32),
        ),
        in_specs=[VM] * 3,
        out_specs=(VM, HBM, VM, VM, VM),
        scratch_shapes=[
            pltpu.VMEM((2 * length - 256, 256), F32),
            pltpu.VMEM((2 * length - 256, 256), F32),
            pltpu.VMEM((2, length, length), BF),
            pltpu.SemaphoreType.DMA((2,)),
        ],
        compiler_params=pltpu.CompilerParams(vmem_limit_bytes=60 << 20),
    )(x, mix, small)


def centre(r):
    c = r - jnp.mean(r, axis=-1, keepdims=True)
    factor = lax.rsqrt(jnp.mean(c * c, axis=-1, keepdims=True) + EPSILON)
    return c * factor, factor


def uncentre(e, n, factor):
    return factor * (e - jnp.mean(e, axis=-1, keepdims=True) - n * jnp.mean(e * n, axis=-1, keepdims=True))


def colsum(v):
    return jnp.sum(v, axis=0, keepdims=True)


def tile(t, size=256):
    return pl.ds(pl.multiple_of(t * size, size), size)


def geglu_kernel(x_ref, att_ref, proj_ref, vec_ref, cs_ref, we_hbm, wc_hbm,
                 res_ref, gr_ref, ga_ref, gproj_ref, gsm_ref, gcon_hbm, gexp_hbm,
                 we, wc, n1, f1, fl, flt, hid, da, du, gd, gcb, geb, wsem, osem):
    length, width = x_ref.shape
    ff = wc.shape[0]
    get_e = pltpu.make_async_copy(we_hbm, we, wsem.at[0])
    get_c = pltpu.make_async_copy(wc_hbm, wc, wsem.at[1])
    get_e.start()
    get_c.start()
    gsm_ref[...] = jnp.zeros_like(gsm_ref)
    offset, mg, ms, cb, fg, fs = (vec_ref[i : i + 1] for i in range(2, 8))
    hid[:, :width] = att_ref[...].T

    def norm_one(b, _):
        rows = tile(b, RB)
        r = product(hid[rows, :width], proj_ref[...]) + offset + x_ref[rows].astype(F32)
        n, factor = centre(r)
        n1[rows] = n
        f1[rows] = factor
        fl[rows] = (n * mg + ms).astype(BF)
        return 0

    lax.fori_loop(0, length // RB, norm_one, 0)
    flt[...] = fl[...].T
    get_e.wait()

    def up(t, _):
        cols = tile(t)
        g = product(fl[...], we[0, :, cols])
        u = product(fl[...], we[1, :, cols])
        cdf = 0.5 + 0.5 * lax.erf(g * 0.7071067811865476)
        pdf = jnp.exp2(g * g * (-0.5 * LOG2E)) * 0.3989422804014327
        ge = g * cdf
        hid[:, cols] = (ge * u).astype(BF)
        du[:, cols] = ge.astype(BF)
        da[:, cols] = (u * (cdf + g * pdf)).astype(BF)
        return 0

    lax.fori_loop(0, ff // 256, up, 0)
    get_c.wait()

    def down(t, _):
        gr_ref[:, tile(t)] = product(hid[...], wc[:, tile(t)])
        return 0

    lax.fori_loop(0, width // 256, down, 0)

    def norm_two(b, _):
        rows = tile(b, RB)
        n, factor = centre(gr_ref[rows] + cb + (n1[rows] * mg + ms))
        res_ref[rows] = (n * fg + fs).astype(BF)
        ct = cs_ref[rows].astype(F32)
        gsm_ref[6:7] += colsum(ct * n)
        gsm_ref[7:8] += colsum(ct)
        g2 = uncentre(ct * fg, n, factor)
        gr_ref[rows] = g2
        gl = g2.astype(BF)
        gd[rows] = gl
        gsm_ref[5:6] += colsum(gl.astype(F32))
        return 0

    lax.fori_loop(0, length // RB, norm_two, 0)

    def out_copies(t, slot):
        return (
            pltpu.make_async_copy(gcb.at[slot], gcon_hbm.at[tile(t)], osem.at[0, slot]),
            pltpu.make_async_copy(geb.at[slot, 0], gexp_hbm.at[0, :, tile(t)], osem.at[1, slot]),
            pltpu.make_async_copy(geb.at[slot, 1], gexp_hbm.at[1, :, tile(t)], osem.at[2, slot]),
        )

    def back(t, _):
        slot = lax.rem(t, 2)
        cols = tile(t)

        @pl.when(t >= 2)
        def _():
            for copy in out_copies(0, slot):
                copy.wait()

        gh = product_nt(gd[...], wc[cols, :])
        gcb[slot] = product_tn(hid[:, cols], gd[...]).astype(BF)
        gg = (gh * da[:, cols].astype(F32)).astype(BF)
        gu = (gh * du[:, cols].astype(F32)).astype(BF)
        da[:, cols] = gg
        du[:, cols] = gu
        geb[slot, 0] = product(flt[...], gg).astype(BF)
        geb[slot, 1] = product(flt[...], gu).astype(BF)
        for copy in out_copies(t, slot):
            copy.start()
        return 0

    lax.fori_loop(0, ff // 256, back, 0)

    def first_back(t, _):
        cols = tile(t)
        gr_ref[:, cols] += product_nt(da[...], we[0, cols, :]) + product_nt(du[...], we[1, cols, :])
        return 0

    lax.fori_loop(0, width // 256, first_back, 0)

    def norm_one_back(b, _):
        rows = tile(b, RB)
        gf = gr_ref[rows]
        n = n1[rows]
        gsm_ref[3:4] += colsum(gf * n)
        gsm_ref[4:5] += colsum(gf)
        g1 = uncentre(gf * mg, n, f1[rows])
        gr_ref[rows] = g1
        gl = g1.astype(BF)
        gd[rows] = gl
        gsm_ref[2:3] += colsum(gl.astype(F32))
        return 0

    lax.fori_loop(0, length // RB, norm_one_back, 0)
    ga_ref[...] = product_nt(proj_ref[...], gd[...]).astype(BF)
    gproj_ref[...] = product(att_ref[...], gd[...]).astype(BF)
    for slot in range(2):
        for copy in out_copies(0, slot):
            copy.wait()


def geglu_both_ways(x, att, proj, vec, cs, we, wc):
    length, width = x.shape
    ff = wc.shape[0]
    return pl.pallas_call(
        geglu_kernel,
        out_shape=(
            SDS((length, width), BF),
            SDS((length, width), F32),
            SDS((width, length), BF),
            SDS((width, width), BF),
            SDS((8, width), F32),
            SDS((ff, width), BF),
            SDS((2, width, ff), BF),
        ),
        in_specs=[VM] * 5 + [HBM] * 2,
        out_specs=(VM,) * 5 + (HBM,) * 2,
        scratch_shapes=[
            pltpu.VMEM((2, width, ff), BF),
            pltpu.VMEM((ff, width), BF),
            pltpu.VMEM((length, width), F32),
            pltpu.VMEM((length, 1), F32),
            pltpu.VMEM((length, width), BF),
            pltpu.VMEM((width, length), BF),
            pltpu.VMEM((length, ff), BF),
            pltpu.VMEM((length, ff), BF),
            pltpu.VMEM((length, ff), BF),
            pltpu.VMEM((length, width), BF),
            pltpu.VMEM((2, 256, width), BF),
            pltpu.VMEM((2, 2, width, 256), BF),
            pltpu.SemaphoreType.DMA((2,)),
            pltpu.SemaphoreType.DMA((3, 2)),
        ],
        compiler_params=pltpu.CompilerParams(vmem_limit_bytes=63 << 20),
    )(x, att, proj, vec, cs, we, wc)


def attend_grad_kernel(x_ref, mix_ref, mixed_ref, linv_ref, ga_ref, att_ref, gr_ref, gin_ref, e_hbm,
                       ig_ref, gmix_ref, gsm_ref, xt, gm, ebuf, ds, esem):
    length, width = x_ref.shape

    def read(head, slot):
        return pltpu.make_async_copy(e_hbm.at[head], ebuf.at[slot], esem.at[slot])

    read(0, 0).start()
    read(1, 1).start()
    gsm_ref[...] = gin_ref[...]
    xt[...] = x_ref[...].T
    lane = lax.broadcasted_iota(jnp.int32, (1, 128), 1)

    def pair(i, _):
        sq = tile(i, 128)
        sk = pl.ds(pl.multiple_of(width + i * 128, 128), 128)
        sv = pl.ds(pl.multiple_of(2 * width + i * 128, 128), 128)
        q = mixed_ref[:, sq]
        k = mixed_ref[:, sk]
        v = mixed_ref[:, sv]
        kt = k.T
        dk = dv = None
        dq = []
        for side in range(2):
            head = 2 * i + side
            rows = tile(head, 64)
            g = (ga_ref[rows, :].astype(F32) * linv_ref[pl.ds(head, 1), :]).astype(BF)
            less = -jnp.sum(g.astype(F32) * att_ref[rows, :].astype(F32), axis=0, keepdims=True)
            high = less.astype(BF)
            low = (less - high.astype(F32)).astype(BF)
            zero = jnp.zeros((64, length), BF)
            row = lax.broadcasted_iota(jnp.int32, (64, length), 0)
            extra = jnp.where(row == 0, high, jnp.where(row == 1, low, zero))
            rhs = jnp.concatenate([g, extra] if side == 0 else [extra, g], axis=0)
            grads = jnp.concatenate([g, zero] if side == 0 else [zero, g], axis=0).T
            mine = (lane < 64) == (side == 0)
            values = jnp.where(mine, v, jnp.ones_like(v))
            queries = jnp.where(mine, q, jnp.zeros_like(q))
            read(0, side).wait()
            for b in range(length // 256):
                cols = slice(b * 256, b * 256 + 256)
                dp = product(values, rhs[:, cols])
                ds[side, :, cols] = (dp * ebuf[side, :, cols].astype(F32)).astype(BF)
            dq.append(product(kt[side * 64 : side * 64 + 64], ds[side]))
            part = product(ebuf[side], grads)
            dv = part if dv is None else dv + part
            part = product(ds[side], queries)
            dk = part if dk is None else dk + part

            @pl.when(i < 5)
            def _():
                read(head + 2, side).start()

        gq = (jnp.concatenate(dq, axis=0) * HEAD_DIM**-0.5).T.astype(BF)
        gk = (dk * (1.0 / LOG2E)).astype(BF)
        gv = dv.astype(BF)
        gm[:, sq] = gq
        gm[:, sk] = gk
        gm[:, sv] = gv
        gsm_ref[0:1, sq] = colsum(gq.astype(F32))
        gsm_ref[1:2, sq] = colsum(gv.astype(F32))
        gmix_ref[:, sq] = product(xt[...], gq).astype(BF)
        gmix_ref[:, sk] = product(xt[...], gk).astype(BF)
        gmix_ref[:, sv] = product(xt[...], gv).astype(BF)
        return 0

    lax.fori_loop(0, 6, pair, 0)

    def last(t, _):
        cols = tile(t)
        ig_ref[:, cols] = (gr_ref[:, cols] + product_nt(gm[...], mix_ref[cols, :])).astype(BF)
        return 0

    lax.fori_loop(0, width // 256, last, 0)


def attend_grad(x, mix, mixed, linv, ga, att, gr, gsm, e):
    length, width = x.shape
    return pl.pallas_call(
        attend_grad_kernel,
        out_shape=(SDS((length, width), BF), SDS((width, 3 * width), BF), SDS((8, width), F32)),
        in_specs=[VM] * 8 + [HBM],
        out_specs=(VM,) * 3,
        scratch_shapes=[
            pltpu.VMEM((width, length), BF),
            pltpu.VMEM((length, 3 * width), BF),
            pltpu.VMEM((2, length, length), BF),
            pltpu.VMEM((2, length, length), BF),
            pltpu.SemaphoreType.DMA((2,)),
        ],
        compiler_params=pltpu.CompilerParams(vmem_limit_bytes=60 << 20),
    )(x, mix, mixed, linv, ga, att, gr, gsm, e)


class Scatter:
    def __init__(self, place, sems, tag, grad, out, r0, own, r1, r2, r3, fin, last, outb):
        self.p, self.sems, self.tag, self.grad, self.out = place, sems, tag, grad, out
        self.r0, self.own, self.r1, self.r2, self.r3, self.fin, self.last, self.outb = r0, own, r1, r2, r3, fin, last, outb
        self.split = r1 is not None
        self.halves = grad.shape[0]
        self.sent = []

    @staticmethod
    def scratch(halves, r, n):
        return [
            pltpu.VMEM((halves, NZ, 2, r, n), BF),
            pltpu.VMEM((halves, NZ, 2, r, n), BF),
        ] + ([pltpu.VMEM((NZ, 2, r, n), BF)] if halves == 2 else []) + [
            pltpu.VMEM((NZ, r, n), BF),
            pltpu.VMEM((NZ, r, n), BF),
            pltpu.VMEM((r, n), BF),
            pltpu.VMEM((r, n), BF),
            pltpu.VMEM((r, halves * n), F32),
        ]

    def send(self, name, arrive, src, dst, to):
        copy = pltpu.make_async_remote_copy(
            src_ref=src,
            dst_ref=dst,
            send_sem=self.sems.at(0, self.tag, *name),
            recv_sem=self.sems.at(1, self.tag, *arrive),
            device_id=to,
            device_id_type=MESH,
        )
        copy.start()
        self.sent.append(copy)

    @property
    def half(self):
        return self.p.x if self.split else 0

    def start(self):
        p = self.p
        self.local = []
        for h in range(self.halves):
            self.send(("s", h), ("s", h), self.grad.at[h, :, :, 1 - p.c], self.r0.at[h], p.sib)
            copy = pltpu.make_async_copy(self.grad.at[h, :, :, p.c], self.own.at[h], self.sems.at(0, self.tag, "own", h))
            copy.start()
            self.local.append(copy)

    def add_core(self):
        p = self.p
        for h in range(self.halves):
            self.local[h].wait()
            landed(self.r0.at[h], self.sems.at(1, self.tag, "s", h))

            def add(i, _):
                a, b = i // 2, lax.rem(i, 2)
                self.r0[h, a, b] = (self.r0[h, a, b].astype(F32) + self.own[h, a, b].astype(F32)).astype(BF)
                return 0

            lax.fori_loop(0, 2 * NZ, add, 0)
        if self.split:
            for z in range(NZ):
                self.send(("x", z), ("x", z), self.r0.at[1 - p.x, z], self.r1.at[z], p.xn)
        else:
            self.send_y()

    def add_x(self):
        p = self.p
        for z in range(NZ):
            landed(self.r1.at[z], self.sems.at(1, self.tag, "x", z))

            def add(b, _):
                self.r0[p.x, z, b] = (self.r0[p.x, z, b].astype(F32) + self.r1[z, b].astype(F32)).astype(BF)
                return 0

            lax.fori_loop(0, 2, add, 0)
        self.send_y()

    def send_y(self):
        p = self.p
        for z in range(NZ):
            self.send(("y", z), ("y", z), self.r0.at[self.half, z, 1 - p.y], self.r2.at[z], p.yn)

    def add_y(self):
        p = self.p
        for z in range(NZ):
            landed(self.r2.at[z], self.sems.at(1, self.tag, "y", z))
            self.r0[self.half, z, p.y] = (self.r0[self.half, z, p.y].astype(F32) + self.r2[z].astype(F32)).astype(BF)
        for k in (2, 1, 3):
            self.send(("z", k), ("z", NZ - k), self.r0.at[self.half, lax.rem(p.z + k, NZ), p.y], self.r3.at[NZ - k], p.zn[k])

    def add_z(self):
        p = self.p
        for k in range(1, NZ):
            landed(self.r3.at[k], self.sems.at(1, self.tag, "z", k))
        total = self.r0[self.half, p.z, p.y].astype(F32)
        for k in range(1, NZ):
            total += self.r3[k].astype(F32)
        self.fin[...] = total.astype(BF)
        self.send(("f",), ("f",), self.fin, self.last, p.xn)

    def finish(self):
        p = self.p
        landed(self.last, self.sems.at(1, self.tag, "f"))
        if self.split:
            n = self.fin.shape[1]
            self.outb[:, pl.ds(pl.multiple_of(p.x * n, 128), n)] = self.fin[...].astype(F32)
            self.outb[:, pl.ds(pl.multiple_of((1 - p.x) * n, 128), n)] = self.last[...].astype(F32)
        else:
            self.outb[...] = self.fin[...].astype(F32) + self.last[...].astype(F32)
        self.written = pltpu.make_async_copy(self.outb, self.out, self.sems.at(0, self.tag, "out"))
        self.written.start()

    def drain(self):
        self.written.wait()
        for copy in self.sent:
            copy.wait_send()


class SumAll:
    def __init__(self, place, sems, tag, src, out, bufs):
        self.p, self.sems, self.tag, self.src, self.out, self.bufs = place, sems, tag, src, out, bufs
        self.sent = []

    def swap(self, name, src, dst, to):
        copy = pltpu.make_async_remote_copy(
            src_ref=src, dst_ref=dst, send_sem=self.sems.at(0, self.tag, name), recv_sem=self.sems.at(1, self.tag, name),
            device_id=to, device_id_type=MESH,
        )
        copy.start()
        self.sent.append(copy)

    def core(self):
        self.swap("s", self.src, self.bufs.at[0], self.p.sib)

    def x(self):
        landed(self.bufs.at[0], self.sems.at(1, self.tag, "s"))
        self.bufs[1] = self.src[...] + self.bufs[0]
        self.swap("x", self.bufs.at[1], self.bufs.at[2], self.p.xn)

    def y(self):
        landed(self.bufs.at[2], self.sems.at(1, self.tag, "x"))
        self.bufs[3] = self.bufs[1] + self.bufs[2]
        self.swap("y", self.bufs.at[3], self.bufs.at[4], self.p.yn)

    def z(self):
        landed(self.bufs.at[4], self.sems.at(1, self.tag, "y"))
        p = self.p
        self.bufs[5 + p.z] = self.bufs[3] + self.bufs[4]
        for k in range(1, NZ):
            copy = pltpu.make_async_remote_copy(
                src_ref=self.bufs.at[5 + p.z], dst_ref=self.bufs.at[5 + p.z],
                send_sem=self.sems.at(0, self.tag, "z", k), recv_sem=self.sems.at(1, self.tag, "z", NZ - k),
                device_id=p.zn[k], device_id_type=MESH,
            )
            copy.start()
            self.sent.append(copy)

    def finish(self):
        p = self.p
        for k in range(1, NZ):
            landed(self.bufs.at[5 + lax.rem(p.z + k, NZ)], self.sems.at(1, self.tag, "z", k))
        total = self.bufs[5]
        for z in range(1, NZ):
            total += self.bufs[5 + z]
        self.out[...] = total
        for copy in self.sent:
            copy.wait_send()


def scatter_kernel(gcon, gexp, gproj, gmix, gsm, res, ig, ocon, oexp, oproj, omix, osm, ores, oig, *scratch):
    scratch = list(scratch)
    sems = Sems(scratch.pop())
    bufs = scratch.pop()
    p = Place()

    def take(tag, grad, out):
        halves = grad.shape[0]
        count = 8 if halves == 2 else 7
        refs = [scratch.pop(0) for _ in range(count)]
        if halves == 1:
            refs.insert(2, None)
        return Scatter(p, sems, tag, grad, out, *refs)

    c = take("contract", gcon, ocon)
    e = take("expand", gexp, oexp)
    r = take("proj", gproj, oproj)
    m = take("mix", gmix, omix)
    small = SumAll(p, sems, "small", gsm, osm, bufs)
    results = SwapBack(p, sems, "res", res, ores)
    igs = SwapBack(p, sems, "ig", ig, oig)
    p.greet()
    order = (e, c, m, r)
    run([g.start for g in order])
    small.core()
    run([e.add_core, c.add_core, m.add_core, r.add_core, small.x, c.add_y, small.y, e.add_x, m.add_y, r.add_y, small.z])
    results.start()
    igs.start()
    run([c.add_z, e.add_y, m.add_z, r.add_z, c.finish, e.add_z, m.finish, r.finish, small.finish, e.finish])
    results.finish()
    igs.finish()
    run([g.drain for g in order])


def scatter(gcon, gexp, gproj, gmix, gsm, res, ig):
    n = lax.axis_size("dp")
    length, width = res.shape
    ff = gcon.shape[0]

    def cut(grad):
        halves, rows, columns = grad.shape
        return grad.reshape(halves, NZ, 2, 2, rows // n, columns)

    grads = [cut(g) for g in (gcon[None], gexp, gproj[None], gmix[None])]
    halves = SDS((2, length // 2, width), BF)
    scratch = []
    for g in grads:
        scratch += Scatter.scratch(g.shape[0], g.shape[4], g.shape[5])
    return pl.pallas_call(
        scatter_kernel,
        out_shape=(
            SDS((ff // n, width), F32),
            SDS((width // n, 2 * ff), F32),
            SDS((width // n, width), F32),
            SDS((width // n, 3 * width), F32),
            SDS((8, width), F32),
            halves,
            halves,
        ),
        in_specs=[HBM] * 4 + [VM] + [HBM] * 2,
        out_specs=(HBM,) * 4 + (VM,) + (HBM,) * 2,
        scratch_shapes=scratch + [pltpu.VMEM((9, 8, width), F32), pltpu.SemaphoreType.DMA((2, 80))],
        compiler_params=pltpu.CompilerParams(
            collective_id=1, has_side_effects=True, vmem_limit_bytes=62 << 20
        ),
    )(*grads, gsm, res, ig)


def body_whole(inputs, cotangent, mixing, query_bias, value_bias, projection, offset, middle_gain, middle_shift,
               expand, contract, contract_bias, final_gain, final_shift):
    width = inputs.shape[2]
    vectors = (query_bias, value_bias, offset, middle_gain, middle_shift, contract_bias, final_gain, final_shift)
    share = query_bias.shape[0]
    at = lax.axis_index("dp") * share
    small = lax.dynamic_update_slice(jnp.zeros((16, width), BF), jnp.stack(vectors), (0, at))
    xs, cs, small_all, mix, we, wc, proj = gather(inputs, cotangent, small, mixing, expand, contract, projection)
    mixed, e, att, linv, vec = attend(xs, mix, small_all)
    res, gr, ga, gproj, gsm, gcon, gexp = geglu_both_ways(xs, att, proj, vec, cs, we, wc)
    ig, gmix, gsm = attend_grad(xs, mix, mixed, linv, ga, att, gr, gsm, e)
    ocon, oexp, oproj, omix, osm, ores, oig = scatter(gcon, gexp, gproj, gmix, gsm, res, ig)
    own = lax.dynamic_slice(osm, (0, at), (8, share))
    return (ores, oig, omix, own[0], own[1], oproj, own[2], own[3], own[4], oexp, ocon, own[5], own[6], own[7])


def solution(mesh):
    placed = (P("dp", "ctx", None),) * 2 + tuple(
        P("dp", None) if rank == 2 else P("dp") for rank in (2, 1, 1, 2, 1, 1, 1, 2, 2, 1, 1, 1)
    )
    whole = mesh.shape["ctx"] == 2 and mesh.shape["dp"] == 4 * NZ
    return jax.shard_map(
        body_whole if whole else body,
        mesh=mesh,
        in_specs=placed,
        out_specs=placed,
        check_vma=False,
    )
```
